512 devices in a mesh: grp: 8 (over z_lo), ent: 64 (over y, z_hi, x, core).
Axes of the slice: x: 4, y: 4, z: 16 (z_hi: 2, z_lo: 8; z = z_hi * 8 + z_lo), core: 2. Of those that a mesh axis runs over, the one named last changes fastest.
Arguments:
- images: bfloat16 [1536, 1024], P(('grp', 'ent')), may hold values from -256 to 256
- texts: bfloat16 [8, 65536, 1024], P('grp', 'ent'), may hold values from -6 to 6
Outputs:
- prototypes: bfloat16 [8, 65536, 1024], P('grp', 'ent')
- mass: float32 [8, 65536], P('grp', 'ent')
The draws below stay inside these ranges and needn't reach their ends.
All inputs are finite; a program needn't handle non-finite values.
Results may differ from the reference program's by a relative error of at most 0.0095.
Values may be sent and summed in bfloat16 or wider, within the bound.
No kernel may reach another device: no remote copies, remote signals or barrier semaphores. Data moves between devices by JAX's collectives and lax.ppermute only.
A program may use at most 64 MiB of HBM per device.

```python
import math
import jax
import jax.numpy as jnp
from jax import lax

D = 1024
ENTRIES = 524288
SLAB = 65536
IMAGES = 1536


def shared_texts(key):
    return jnp.clip(jax.random.normal(key, (ENTRIES, D), jnp.float32), -6.0, 6.0)


def draw_texts(key, part):
    base = shared_texts(key)
    return base.reshape(-1, SLAB, D).astype(jnp.bfloat16)


def draw_images(key, part):
    base = shared_texts(key)
    key = jax.random.fold_in(key, 2)
    first, second = jax.random.split(key)
    scale = jnp.exp(jax.random.uniform(second, (IMAGES, 1), jnp.float32, jnp.log(0.6), jnp.log(1.6)))
    rows = jnp.clip(jax.random.normal(first, (IMAGES, D), jnp.float32), -6.0, 6.0) * scale
    strengths = jnp.array([40.0, 60.0, 90.0, 120.0], jnp.float32) / math.sqrt(D)
    aligned = strengths[:, None] * (base[ENTRIES - 4:] + 0.99 * base[ENTRIES - 8:ENTRIES - 4])
    rows = rows.at[:4].set(aligned)
    return jnp.clip(rows, -256.0, 256.0).astype(jnp.bfloat16)


def setup_inputs(seed: int = 0) -> dict:
    seeds = jax.random.split(jax.random.key(seed), 3)
    return {
        "images": draw_images(jax.random.fold_in(seeds[2], 71), 0),
        "texts": draw_texts(jax.random.fold_in(seeds[2], 71), 0),
    }


sharpness = 3.0

def reference(images, texts):
    factor = sharpness / math.sqrt(D)

    def scores_of(slab):
        return jnp.dot(images, slab.T, preferred_element_type=jnp.float32) * factor

    def online(carry, slab):
        peak, total = carry
        scores = scores_of(slab)
        newpeak = jnp.maximum(peak, lax.optimization_barrier(jnp.max(scores, axis=1)))
        total = total * jnp.exp(peak - newpeak) + lax.optimization_barrier(jnp.sum(jnp.exp(scores - newpeak[:, None]), axis=1))
        return ((newpeak, total), None)
    start = (jnp.full((images.shape[0],), -jnp.inf, jnp.float32), jnp.zeros((images.shape[0],), jnp.float32))
    (peak, total), unused = lax.scan(online, start, texts)

    def per_slab(slab):
        scores = scores_of(slab)
        weights = (jnp.exp(scores - peak[:, None]) / total[:, None]).astype(jnp.bfloat16)
        column = lax.optimization_barrier(jnp.sum(weights.astype(jnp.float32), axis=0))
        summed = jnp.dot(weights.T, images, preferred_element_type=jnp.float32)
        return ((summed / column[:, None]).astype(jnp.bfloat16), column * (ENTRIES / IMAGES))
    prototypes, mass = lax.map(per_slab, texts)
    return (prototypes, mass)
```

```python
import math

import jax
import jax.numpy as jnp
import numpy as np
from jax import lax
from jax.sharding import Mesh, PartitionSpec as P

sharpness = 3.0

AXES = ("zl", "y", "zh", "x", "c")
SIZES = (8, 4, 2, 4, 2)
Z = ("zh", "zl")
PLANE = ("y", "x")
NEAR = ("y", "x", "c")


def count(axes):
    return math.prod(SIZES[AXES.index(a)] for a in axes)


def spread(block, axes):
    n = count(axes)
    copies = lax.optimization_barrier(jnp.broadcast_to(block[None], (n,) + block.shape))
    return lax.all_to_all(copies, axes, 0, 0, tiled=True)


def merge(lse, axes):
    got = spread(lse, axes)
    top = jnp.max(got, axis=0)
    return top + jnp.log(jnp.sum(jnp.exp(got - top[None]), axis=0))


def shards(images, texts):
    rows, width = images.shape
    factor = sharpness / math.sqrt(width)
    slab_rows = texts[0]
    block = slab_rows.shape[0]
    n = count(AXES) * rows
    mass_scale = block * count(AXES) / n
    mine = spread(images.reshape(-1, 128), Z).reshape(-1, 128)
    mine = spread(mine, PLANE).reshape(-1, width)
    other = lax.ppermute(mine, "c", [(0, 1), (1, 0)])
    gathered = jnp.concatenate([mine, other], axis=0)
    scores = jnp.dot(slab_rows, gathered.T, preferred_element_type=jnp.float32) * factor
    local_peak = jnp.max(scores, axis=0)
    local_total = jnp.sum(jnp.exp(scores - local_peak[None]), axis=0)
    lse = (local_peak + jnp.log(local_total)).reshape(2, -1, 128)
    core = lax.axis_index("c")
    lse = jnp.where(core == 0, lse, lse[::-1])
    lse = merge(merge(lse, NEAR), Z)
    lse = jnp.where(core == 0, lse, lse[::-1]).reshape(-1)
    weights = jnp.exp(scores - lse[None]).astype(jnp.bfloat16)
    column = jnp.sum(weights.astype(jnp.float32), axis=1)
    summed = jnp.dot(weights, gathered, preferred_element_type=jnp.float32)
    prototypes = (summed / column[:, None]).astype(jnp.bfloat16)
    mass = column * mass_scale
    return (prototypes[None], mass[None])


def solution(mesh):
    fine = Mesh(np.asarray(mesh.devices).reshape(SIZES), AXES)
    grp, ent = AXES[:1], AXES[1:]
    return jax.shard_map(
        shards,
        mesh=fine,
        in_specs=(P(AXES, None), P(grp, ent, None)),
        out_specs=(P(grp, ent, None), P(grp, ent)),
        check_vma=False,
    )
```

```python
import functools
import math

import jax
import jax.numpy as jnp
import numpy as np
from jax import lax
from jax.experimental import pallas as pl
from jax.experimental.pallas import tpu as pltpu
from jax.sharding import Mesh, PartitionSpec as P

sharpness = 3.0

AXES = ("zl", "y", "zh", "x", "c")
SIZES = (8, 4, 2, 4, 2)
Z = ("zh", "zl")
PLANE = ("y", "x")
NEAR = ("y", "x", "c")
WHOLE = pl.BlockSpec(memory_space=pltpu.VMEM)
PARAMS = pltpu.CompilerParams(vmem_limit_bytes=48 << 20)


def count(axes):
    return math.prod(SIZES[AXES.index(a)] for a in axes)


def spread(block, axes):
    n = count(axes)
    copies = lax.optimization_barrier(jnp.broadcast_to(block[None], (n,) + block.shape))
    return lax.all_to_all(copies, axes, 0, 0, tiled=True)


def merge(lse, axes):
    got = spread(lse, axes)
    top = jnp.max(got, axis=0)
    return top + jnp.log(jnp.sum(jnp.exp(got - top[None]), axis=0))


def scores_kernel(factor, texts, images, shares, stats):
    dots = lax.dot_general(texts[...], images[...], (((1,), (1,)), ((), ())), preferred_element_type=jnp.float32)
    top = jnp.max(dots, axis=0, keepdims=True)
    parts = jnp.exp2((dots - top) * (factor * math.log2(math.e)))
    shares[...] = parts.astype(jnp.bfloat16)
    stats[0:1] = top * factor
    stats[1:2] = top * factor + jnp.log(jnp.sum(parts, axis=0, keepdims=True))


def scores(texts, images, factor):
    (entries, width), n = texts.shape, images.shape[0]
    return pl.pallas_call(
        functools.partial(scores_kernel, factor),
        out_shape=[jax.ShapeDtypeStruct((entries, n), jnp.bfloat16), jax.ShapeDtypeStruct((2, n), jnp.float32)],
        in_specs=[WHOLE] * 2,
        out_specs=[WHOLE] * 2,
        compiler_params=PARAMS,
        name="scores",
        cost_estimate=pl.CostEstimate(flops=2 * entries * width * n, bytes_accessed=2 * (entries * width + n * width + entries * n), transcendentals=entries * n),
    )(texts, images)


def prototypes_kernel(mass_scale, shares_a, shares_b, scale_a, scale_b, images_a, images_b, out, mass):
    weights_a = (shares_a[...].astype(jnp.float32) * scale_a[...]).astype(jnp.bfloat16)
    weights_b = (shares_b[...].astype(jnp.float32) * scale_b[...]).astype(jnp.bfloat16)
    lanes = None
    for weights in (weights_a, weights_b):
        for j in range(0, weights.shape[1], 128):
            part = weights[:, j : j + 128].astype(jnp.float32)
            lanes = part if lanes is None else lanes + part
    summed = jnp.dot(weights_a, images_a[...], preferred_element_type=jnp.float32)
    summed += jnp.dot(weights_b, images_b[...], preferred_element_type=jnp.float32)
    out[0] = (summed / jnp.sum(lanes, axis=1, keepdims=True)).astype(jnp.bfloat16)
    mass[...] = jnp.sum(lanes.T, axis=0, keepdims=True) * mass_scale


def prototypes(shares, scales, images, mass_scale, steps=2):
    (entries, n), width = shares[0].shape, images[0].shape[1]
    rows = entries // steps
    return pl.pallas_call(
        functools.partial(prototypes_kernel, mass_scale),
        grid=(steps,),
        out_shape=[jax.ShapeDtypeStruct((1, entries, width), jnp.bfloat16), jax.ShapeDtypeStruct((1, entries), jnp.float32)],
        in_specs=[pl.BlockSpec((rows, n), lambda i: (i, 0))] * 2 + [WHOLE] * 4,
        out_specs=[pl.BlockSpec((1, rows, width), lambda i: (0, i, 0)), pl.BlockSpec((1, rows), lambda i: (0, i))],
        compiler_params=PARAMS,
        name="prototypes",
        cost_estimate=pl.CostEstimate(flops=4 * entries * width * n, bytes_accessed=4 * (entries * width + n * width + entries * n), transcendentals=0),
    )(*shares, *scales, *images)


def shards(images, texts):
    rows, width = images.shape
    factor = sharpness / math.sqrt(width)
    slab_rows = texts[0]
    block = slab_rows.shape[0]
    n = count(AXES) * rows
    mass_scale = block * count(AXES) / n
    line = spread(images.reshape(-1, 128), Z).reshape(-1, width)
    mine = spread(line, PLANE).reshape(-1, width)
    other = lax.ppermute(mine, "c", [(0, 1), (1, 0)])
    shares_a, stats_a = scores(slab_rows, mine, factor)
    shares_b, stats_b = scores(slab_rows, other, factor)
    core = lax.axis_index("c")
    lse_a, lse_b = stats_a[1].reshape(1, -1, 128), stats_b[1].reshape(1, -1, 128)
    lse = jnp.concatenate([jnp.where(core == 0, lse_a, lse_b), jnp.where(core == 0, lse_b, lse_a)])
    lse = merge(merge(lse, NEAR), Z).reshape(2, 1, -1)
    scale_a = jnp.exp(stats_a[0:1] - jnp.where(core == 0, lse[0], lse[1]))
    scale_b = jnp.exp(stats_b[0:1] - jnp.where(core == 0, lse[1], lse[0]))
    return prototypes((shares_a, shares_b), (scale_a, scale_b), (mine, other), mass_scale)


def solution(mesh):
    fine = Mesh(np.asarray(mesh.devices).reshape(SIZES), AXES)
    grp, ent = AXES[:1], AXES[1:]
    return jax.shard_map(
        shards,
        mesh=fine,
        in_specs=(P(AXES, None), P(grp, ent, None)),
        out_specs=(P(grp, ent, None), P(grp, ent)),
        check_vma=False,
    )
```

```python
import functools
import math

import jax
import jax.numpy as jnp
import numpy as np
from jax import lax
from jax.experimental import pallas as pl
from jax.experimental.pallas import tpu as pltpu
from jax.sharding import Mesh, PartitionSpec as P

sharpness = 3.0

AXES = ("zl", "y", "zh", "x", "c")
SIZES = (8, 4, 2, 4, 2)
Z = ("zh", "zl")
PLANE = ("y", "x")
NEAR = ("y", "x", "c")
SWAP = [(0, 1), (1, 0)]
WHOLE = pl.BlockSpec(memory_space=pltpu.VMEM)
bf16, f32 = jnp.bfloat16, jnp.float32
struct = jax.ShapeDtypeStruct


def count(axes):
    return math.prod(SIZES[AXES.index(a)] for a in axes)


def params(mib):
    return pltpu.CompilerParams(vmem_limit_bytes=mib << 20)


def exchange(copies, axes):
    return lax.all_to_all(copies, axes, 0, 0, tiled=True)


def spread(block, axes):
    n = count(axes)
    return exchange(lax.optimization_barrier(jnp.broadcast_to(block[None], (n,) + block.shape)), axes)


def merge(parts):
    top = jnp.max(parts, axis=0)
    return top + jnp.log(jnp.sum(jnp.exp(parts - top[None]), axis=0))


def scores_kernel(factor, texts, images, *refs):
    before, (shares, peak, lse) = refs[:-3], refs[-3:]
    dots = lax.dot_general(texts[...], images[...], (((1,), (1,)), ((), ())), preferred_element_type=f32)
    top = jnp.max(dots, axis=0, keepdims=True)
    parts = jnp.exp2((dots - top) * (factor * math.log2(math.e)))
    shares[...] = parts.astype(bf16)
    peak[...] = top * factor
    here = top * factor + jnp.log(jnp.sum(parts, axis=0, keepdims=True))
    if before:
        core, shape = lax.axis_index("c"), (lse.shape[0], 1) + here.shape
        lse[:, pl.ds(core, 1)] = jnp.broadcast_to(before[0][...], shape)
        lse[:, pl.ds(1 - core, 1)] = jnp.broadcast_to(here, shape)
    else:
        lse[...] = here


def scores(texts, images, factor, before=(), copies=None):
    (entries, width), n = texts.shape, images.shape[0]
    return pl.pallas_call(
        functools.partial(scores_kernel, factor),
        out_shape=[struct((entries, n), bf16), struct((1, n), f32), struct((copies, 2, 1, n) if before else (1, n), f32)],
        in_specs=[WHOLE] * (2 + len(before)),
        out_specs=[WHOLE] * 3,
        compiler_params=params(12),
        name="scores",
        cost_estimate=pl.CostEstimate(flops=2 * entries * width * n, bytes_accessed=2 * (entries * width + n * width + entries * n), transcendentals=entries * n),
    )(texts, images, *before)


def merge_kernel(parts, out):
    out[...] = jnp.broadcast_to(merge(parts[...])[None], out.shape)


def merged(parts, copies):
    return pl.pallas_call(
        merge_kernel,
        out_shape=struct((copies,) + parts.shape[1:], f32),
        in_specs=[WHOLE],
        out_specs=WHOLE,
        compiler_params=params(4),
        name="merge",
        cost_estimate=pl.CostEstimate(flops=4 * parts.size, bytes_accessed=8 * parts.size, transcendentals=parts.size),
    )(parts)


def prototypes_kernel(mass_scale, shares_own, shares_other, parts, peak_own, peak_other, images_own, images_other, out, mass):
    core = lax.axis_index("c")
    lanes = summed = None
    for shares, images, peak, at in ((shares_own, images_own, peak_own, core), (shares_other, images_other, peak_other, 1 - core)):
        scale = jnp.exp(peak[...] - merge(parts[:, pl.ds(at, 1)])[0])
        weights = (shares[...].astype(f32) * scale).astype(bf16)
        for j in range(0, weights.shape[1], 128):
            part = weights[:, j : j + 128].astype(f32)
            lanes = part if lanes is None else lanes + part
        product = jnp.dot(weights, images[...], preferred_element_type=f32)
        summed = product if summed is None else summed + product
    out[0] = (summed * (1.0 / jnp.sum(lanes, axis=1, keepdims=True))).astype(bf16)
    mass[...] = jnp.sum(lanes.T, axis=0, keepdims=True) * mass_scale


def prototypes(shares, parts, peaks, images, mass_scale, steps=2):
    (entries, n), width = shares[0].shape, images[0].shape[1]
    rows = entries // steps
    return pl.pallas_call(
        functools.partial(prototypes_kernel, mass_scale),
        grid=(steps,),
        out_shape=[struct((1, entries, width), bf16), struct((1, entries), f32)],
        in_specs=[pl.BlockSpec((rows, n), lambda i: (i, 0))] * 2 + [WHOLE] * 5,
        out_specs=[pl.BlockSpec((1, rows, width), lambda i: (0, i, 0)), pl.BlockSpec((1, rows), lambda i: (0, i))],
        compiler_params=params(24),
        name="prototypes",
        cost_estimate=pl.CostEstimate(flops=4 * entries * width * n, bytes_accessed=2 * (entries * width + 2 * n * width + 2 * entries * n), transcendentals=0),
    )(*shares, parts, *peaks, *images)


def shards(images, texts):
    rows, width = images.shape
    factor = sharpness / math.sqrt(width)
    own = texts[0]
    mass_scale = own.shape[0] / rows
    line = spread(images.reshape(-1, 128), Z).reshape(-1, width)
    mine = spread(line, PLANE).reshape(-1, width)
    other = lax.ppermute(mine, "c", SWAP)
    shares_own, peak_own, lse = scores(own, mine, factor)
    shares_other, peak_other, lse = scores(own, other, factor, (lse,), count(NEAR))
    parts = exchange(merged(exchange(lse, NEAR), count(Z)), Z)
    return prototypes((shares_own, shares_other), parts, (peak_own, peak_other), (mine, other), mass_scale)


def solution(mesh):
    fine = Mesh(np.asarray(mesh.devices).reshape(SIZES), AXES)
    grp, ent = AXES[:1], AXES[1:]
    return jax.shard_map(
        shards,
        mesh=fine,
        in_specs=(P(AXES, None), P(grp, ent, None)),
        out_specs=(P(grp, ent, None), P(grp, ent)),
        check_vma=False,
    )
```

```python
import functools
import math

import jax
import jax.numpy as jnp
import numpy as np
from jax import lax
from jax.experimental import pallas as pl
from jax.experimental.pallas import tpu as pltpu
from jax.sharding import Mesh, PartitionSpec as P

sharpness = 3.0

LATE_Z, LATE_XY = 10, 2
AXES = ("zl", "y", "zh", "x", "c")
SIZES = (8, 4, 2, 4, 2)
Z = ("zh", "zl")
NEAR = ("y", "x", "c")
SWAP = [(0, 1), (1, 0)]
WHOLE = pl.BlockSpec(memory_space=pltpu.VMEM)
bf16, f32 = jnp.bfloat16, jnp.float32
struct = jax.ShapeDtypeStruct


def count(axes):
    return math.prod(SIZES[AXES.index(a)] for a in axes)


def params(mib):
    return pltpu.CompilerParams(vmem_limit_bytes=mib << 20)


def line_groups(first):
    at = np.arange(math.prod(SIZES)).reshape(SIZES)
    lines = at.transpose(1, 3, 4, 2, 0).reshape(-1, count(Z))
    return np.roll(lines, -first, axis=1).tolist()


def plane_groups(first, cores):
    at = np.arange(math.prod(SIZES)).reshape(SIZES)
    planes = at.transpose((0, 2, 1, 3, 4) if cores == 2 else (0, 2, 4, 1, 3)).reshape(-1, 4, 4, cores)
    return np.roll(planes, (-first, -first), axis=(1, 2)).reshape(-1, 16 * cores).tolist()


def exchange(copies, axes, groups=None):
    return lax.all_to_all(copies, axes, 0, 0, tiled=True, axis_index_groups=groups)


def spread(block, axes, groups=None):
    n = len(groups[0]) if groups else count(axes)
    return exchange(lax.optimization_barrier(jnp.broadcast_to(block[None], (n,) + block.shape)), axes, groups)


def merge(parts):
    top = jnp.max(parts, axis=0)
    return top + jnp.log(jnp.sum(jnp.exp(parts - top[None]), axis=0))


def scores_kernel(factor, texts, images, *refs):
    before, (shares, peak, lse) = refs[:-3], refs[-3:]
    dots = lax.dot_general(texts[...], images[...], (((1,), (1,)), ((), ())), preferred_element_type=f32)
    top = jnp.max(dots, axis=0, keepdims=True)
    parts = jnp.exp2((dots - top) * (factor * math.log2(math.e)))
    shares[...] = parts.astype(bf16)
    peak[...] = top * factor
    here = top * factor + jnp.log(jnp.sum(parts, axis=0, keepdims=True))
    if before:
        core, shape = lax.axis_index("c"), (lse.shape[0], 1) + here.shape
        lse[:, pl.ds(core, 1)] = jnp.broadcast_to(before[0][...], shape)
        lse[:, pl.ds(1 - core, 1)] = jnp.broadcast_to(here, shape)
    else:
        lse[...] = here


def scores(texts, images, factor, before=(), copies=None):
    (entries, width), n = texts.shape, images.shape[0]
    return pl.pallas_call(
        functools.partial(scores_kernel, factor),
        out_shape=[struct((entries, n), bf16), struct((1, n), f32), struct((copies, 2, 1, n) if before else (1, n), f32)],
        in_specs=[WHOLE] * (2 + len(before)),
        out_specs=[WHOLE] * 3,
        compiler_params=params(12),
        name="scores",
        cost_estimate=pl.CostEstimate(flops=2 * entries * width * n, bytes_accessed=2 * (entries * width + n * width + entries * n), transcendentals=entries * n),
    )(texts, images, *before)


def merge_kernel(parts, out):
    out[...] = jnp.broadcast_to(merge(parts[...])[None], out.shape)


def merged(parts, copies):
    return pl.pallas_call(
        merge_kernel,
        out_shape=struct((copies,) + parts.shape[1:], f32),
        in_specs=[WHOLE],
        out_specs=WHOLE,
        compiler_params=params(4),
        name="merge",
        cost_estimate=pl.CostEstimate(flops=4 * parts.size, bytes_accessed=8 * parts.size, transcendentals=parts.size),
    )(parts)


def prototypes_kernel(mass_scale, shares_own, shares_other, parts, peak_own, peak_other, images_own, images_other, out, mass):
    core = lax.axis_index("c")
    lanes = summed = None
    for shares, images, peak, at in ((shares_own, images_own, peak_own, core), (shares_other, images_other, peak_other, 1 - core)):
        scale = jnp.exp(peak[...] - merge(parts[:, pl.ds(at, 1)])[0])
        weights = (shares[...].astype(f32) * scale).astype(bf16)
        for j in range(0, weights.shape[1], 128):
            part = weights[:, j : j + 128].astype(f32)
            lanes = part if lanes is None else lanes + part
        product = jnp.dot(weights, images[...], preferred_element_type=f32)
        summed = product if summed is None else summed + product
    out[0] = (summed * (1.0 / jnp.sum(lanes, axis=1, keepdims=True))).astype(bf16)
    mass[...] = jnp.sum(lanes.T, axis=0, keepdims=True) * mass_scale


def prototypes(shares, parts, peaks, images, mass_scale, steps=2):
    (entries, n), width = shares[0].shape, images[0].shape[1]
    rows = entries // steps
    return pl.pallas_call(
        functools.partial(prototypes_kernel, mass_scale),
        grid=(steps,),
        out_shape=[struct((1, entries, width), bf16), struct((1, entries), f32)],
        in_specs=[pl.BlockSpec((rows, n), lambda i: (i, 0))] * 2 + [WHOLE] * 5,
        out_specs=[pl.BlockSpec((1, rows, width), lambda i: (0, i, 0)), pl.BlockSpec((1, rows), lambda i: (0, i))],
        compiler_params=params(24),
        name="prototypes",
        cost_estimate=pl.CostEstimate(flops=4 * entries * width * n, bytes_accessed=2 * (entries * width + 2 * n * width + 2 * entries * n), transcendentals=0),
    )(*shares, parts, *peaks, *images)


def shards(images, texts):
    rows, width = images.shape
    factor = sharpness / math.sqrt(width)
    own = texts[0]
    mass_scale = own.shape[0] / rows
    line = spread(images.reshape(-1, 128), AXES, line_groups(LATE_Z)).reshape(-1, width)
    mine = spread(line, AXES, plane_groups(LATE_XY, 1)).reshape(-1, width)
    other = lax.ppermute(mine, "c", SWAP)
    shares_own, peak_own, lse = scores(own, mine, factor)
    shares_other, peak_other, lse = scores(own, other, factor, (lse,), count(NEAR))
    parts = exchange(merged(exchange(lse, AXES, plane_groups(LATE_XY, 2)), count(Z)), AXES, line_groups(LATE_Z))
    return prototypes((shares_own, shares_other), parts, (peak_own, peak_other), (mine, other), mass_scale)


def solution(mesh):
    fine = Mesh(np.asarray(mesh.devices).reshape(SIZES), AXES)
    grp, ent = AXES[:1], AXES[1:]
    return jax.shard_map(
        shards,
        mesh=fine,
        in_specs=(P(AXES, None), P(grp, ent, None)),
        out_specs=(P(grp, ent, None), P(grp, ent)),
        check_vma=False,
    )
```

```python
import functools
import math

import jax
import jax.numpy as jnp
import numpy as np
from jax import lax
from jax.experimental import pallas as pl
from jax.experimental.pallas import tpu as pltpu
from jax.sharding import Mesh, PartitionSpec as P

sharpness = 3.0

LATE_Z, LATE_XY = 10, 2
AXES = ("zl", "y", "zh", "x", "c")
SIZES = (8, 4, 2, 4, 2)
Z = ("zh", "zl")
NEAR = ("y", "x", "c")
SWAP = [(0, 1), (1, 0)]
WHOLE = pl.BlockSpec(memory_space=pltpu.VMEM)
bf16, f32 = jnp.bfloat16, jnp.float32
struct = jax.ShapeDtypeStruct


def count(axes):
    return math.prod(SIZES[AXES.index(a)] for a in axes)


def params(mib):
    return pltpu.CompilerParams(vmem_limit_bytes=mib << 20)


def line_groups(first):
    at = np.arange(math.prod(SIZES)).reshape(SIZES)
    lines = at.transpose(1, 3, 4, 2, 0).reshape(-1, count(Z))
    return np.roll(lines, -first, axis=1).tolist()


def plane_groups(first, cores):
    at = np.arange(math.prod(SIZES)).reshape(SIZES)
    planes = at.transpose((0, 2, 1, 3, 4) if cores == 2 else (0, 2, 4, 1, 3)).reshape(-1, 4, 4, cores)
    return np.roll(planes, (-first, -first), axis=(1, 2))[..., ::-1].reshape(-1, 16 * cores).tolist()


def exchange(copies, axes, groups=None):
    return lax.all_to_all(copies, axes, 0, 0, tiled=True, axis_index_groups=groups)


def spread(block, axes, groups=None):
    n = len(groups[0]) if groups else count(axes)
    return exchange(lax.optimization_barrier(jnp.broadcast_to(block[None], (n,) + block.shape)), axes, groups)


def merge(parts):
    top = jnp.max(parts, axis=0)
    return top + jnp.log(jnp.sum(jnp.exp(parts - top[None]), axis=0))


def scores_kernel(factor, texts, images, *refs):
    before, (shares, peak, lse) = refs[:-3], refs[-3:]
    dots = lax.dot_general(texts[...], images[...], (((1,), (1,)), ((), ())), preferred_element_type=f32)
    top = jnp.max(dots, axis=0, keepdims=True)
    parts = jnp.exp2((dots - top) * (factor * math.log2(math.e)))
    shares[...] = parts.astype(bf16)
    peak[...] = top * factor
    here = top * factor + jnp.log(jnp.sum(parts, axis=0, keepdims=True))
    if before:
        core, shape = lax.axis_index("c"), (lse.shape[0], 1) + here.shape
        lse[:, pl.ds(core, 1)] = jnp.broadcast_to(before[0][...], shape)
        lse[:, pl.ds(1 - core, 1)] = jnp.broadcast_to(here, shape)
    else:
        lse[...] = here


def scores(texts, images, factor, before=(), copies=None):
    (entries, width), n = texts.shape, images.shape[0]
    return pl.pallas_call(
        functools.partial(scores_kernel, factor),
        out_shape=[struct((entries, n), bf16), struct((1, n), f32), struct((copies, 2, 1, n) if before else (1, n), f32)],
        in_specs=[WHOLE] * (2 + len(before)),
        out_specs=[WHOLE] * 3,
        compiler_params=params(12),
        name="scores",
        cost_estimate=pl.CostEstimate(flops=2 * entries * width * n, bytes_accessed=2 * (entries * width + n * width + entries * n), transcendentals=entries * n),
    )(texts, images, *before)


def merge_kernel(parts, out):
    out[...] = jnp.broadcast_to(merge(parts[...])[None], out.shape)


def merged(parts, copies):
    return pl.pallas_call(
        merge_kernel,
        out_shape=struct((copies,) + parts.shape[1:], f32),
        in_specs=[WHOLE],
        out_specs=WHOLE,
        compiler_params=params(4),
        name="merge",
        cost_estimate=pl.CostEstimate(flops=4 * parts.size, bytes_accessed=8 * parts.size, transcendentals=parts.size),
    )(parts)


def prototypes_kernel(mass_scale, shares_own, shares_other, parts, peak_own, peak_other, images_own, images_other, out, mass):
    core = lax.axis_index("c")
    lanes = summed = None
    for shares, images, peak, at in ((shares_own, images_own, peak_own, core), (shares_other, images_other, peak_other, 1 - core)):
        scale = jnp.exp(peak[...] - merge(parts[:, pl.ds(at, 1)])[0])
        weights = (shares[...].astype(f32) * scale).astype(bf16)
        for j in range(0, weights.shape[1], 128):
            part = weights[:, j : j + 128].astype(f32)
            lanes = part if lanes is None else lanes + part
        product = jnp.dot(weights, images[...], preferred_element_type=f32)
        summed = product if summed is None else summed + product
    out[0] = (summed * (1.0 / jnp.sum(lanes, axis=1, keepdims=True))).astype(bf16)
    mass[...] = jnp.sum(lanes.T, axis=0, keepdims=True) * mass_scale


def prototypes(shares, parts, peaks, images, mass_scale, steps=2):
    (entries, n), width = shares[0].shape, images[0].shape[1]
    rows = entries // steps
    return pl.pallas_call(
        functools.partial(prototypes_kernel, mass_scale),
        grid=(steps,),
        out_shape=[struct((1, entries, width), bf16), struct((1, entries), f32)],
        in_specs=[pl.BlockSpec((rows, n), lambda i: (i, 0))] * 2 + [WHOLE] * 5,
        out_specs=[pl.BlockSpec((1, rows, width), lambda i: (0, i, 0)), pl.BlockSpec((1, rows), lambda i: (0, i))],
        compiler_params=params(24),
        name="prototypes",
        cost_estimate=pl.CostEstimate(flops=4 * entries * width * n, bytes_accessed=2 * (entries * width + 2 * n * width + 2 * entries * n), transcendentals=0),
    )(*shares, parts, *peaks, *images)


def shards(images, texts):
    rows, width = images.shape
    factor = sharpness / math.sqrt(width)
    own = texts[0]
    mass_scale = own.shape[0] / rows
    line = spread(images.reshape(-1, 128), AXES, line_groups(LATE_Z)).reshape(-1, width)
    mine = spread(line, AXES, plane_groups(LATE_XY, 1)).reshape(-1, width)
    other = lax.ppermute(mine, "c", SWAP)
    shares_own, peak_own, lse = scores(own, mine, factor)
    shares_other, peak_other, lse = scores(own, other, factor, (lse,), count(NEAR))
    parts = exchange(merged(exchange(lse, AXES, plane_groups(LATE_XY, 2)), count(Z)), AXES, line_groups(LATE_Z))
    return prototypes((shares_own, shares_other), parts, (peak_own, peak_other), (mine, other), mass_scale)


def solution(mesh):
    fine = Mesh(np.asarray(mesh.devices).reshape(SIZES), AXES)
    grp, ent = AXES[:1], AXES[1:]
    return jax.shard_map(
        shards,
        mesh=fine,
        in_specs=(P(AXES, None), P(grp, ent, None)),
        out_specs=(P(grp, ent, None), P(grp, ent)),
        check_vma=False,
    )
```
